256 devices in a mesh: front: 2 (over core), row: 16 (over y, x), col: 8 (over z).
Axes of the slice: x: 4, y: 4, z: 8, core: 2. Of those that a mesh axis runs over, the one named last changes fastest.
Arguments:
- children: float32 [2, 12288, 12288], P('front', 'row', 'col'), as said below
- pivot_inverse: bfloat16 [2, 3, 1024, 1024], P('front', None, 'row'), as said below
- parent_front: float32 [12288, 12288], P(('front', 'row'), 'col'), may hold values from -1.5 to 1.5
- child_map: int32 [2, 9216], replicated, may hold values from 0 to 12287, as said below
Outputs:
- parent_out: float32 [12288, 12288], P(('front', 'row'), 'col')
- factor: bfloat16 [2, 12288, 3072], P('front', 'row', 'col')
The draws below stay inside these ranges and needn't reach their ends.
Inputs may be any that keep to these rules, and one draw needn't show every extreme that they name: Each row child_map[k] is injective. Say child index u lies in grid row (u // 64) mod 16 and grid column (u // 128) mod 8, and parent index v lies in row block v // 384 and column block v // 1536. Of one grid row's child indices at most 27 map into one row block, and this is reached in every draw; of one grid column's child indices exactly 144 map into each column block. Each children[k] is symmetric positive definite in logical order. Each pivot_inverse[k, p] is lower triangular.
All inputs are finite; a program needn't handle non-finite values.
Results may differ from the reference program's by a relative error of at most 0.0081.
Values may be sent and summed in bfloat16 or wider, within the bound.
A program may use at most 128 MiB of HBM per device.

```python
import math
import jax
import jax.numpy as jnp
from jax import lax

F = 12288
P_SIZE = 1024
NPAN = 3
M = 12288
S = 3072
U = 9216
N_ROW = 16
N_COL = 8


def to_stored_drawn(logical, groups, dimension):
    length = logical.shape[dimension]
    leading = jnp.moveaxis(logical, dimension, 0)
    trailing = leading.shape[1:]
    leading = leading.reshape((length // P_SIZE, groups, P_SIZE // groups) + trailing)
    leading = jnp.swapaxes(leading, 0, 1).reshape((length,) + trailing)
    return jnp.moveaxis(leading, 0, dimension)


def draw_children(key, part):
    key = jax.random.fold_in(key, 5)
    inner = F // 4
    members = []
    for sibling in range(2):
        subkey = jax.random.fold_in(key, sibling)
        first_key, second_key = jax.random.split(subkey, 2)
        factors = jax.random.normal(first_key, (F, inner), jnp.float32)
        coupling = jnp.dot(factors, factors.T, precision=lax.Precision.HIGHEST, preferred_element_type=jnp.float32) * (2.0 / inner)
        coupling = 0.5 * (coupling + coupling.T)
        diagonal = jax.random.uniform(second_key, (F,), jnp.float32, 0.5, 1.5)
        matrix = coupling + jnp.diag(diagonal)
        members.append(to_stored_drawn(to_stored_drawn(matrix, N_ROW, 0), N_COL, 1))
    return jnp.stack(members)


def draw_pivot_inverse(key, part):
    key = jax.random.fold_in(key, 7)
    diag_key, lower_key = jax.random.split(key)
    diagonal = jax.random.uniform(diag_key, (2, NPAN, P_SIZE), jnp.float32, 0.4, 0.7)
    lower = jax.random.normal(lower_key, (2, NPAN, P_SIZE, P_SIZE), jnp.float32) * (0.35 / math.sqrt(P_SIZE))
    rows = jnp.arange(P_SIZE, dtype=jnp.int32)
    strict = (rows[:, None] > rows[None, :]).astype(jnp.float32)
    eye = (rows[:, None] == rows[None, :]).astype(jnp.float32)
    return (lower * strict + diagonal[..., None] * eye).astype(jnp.bfloat16)


def draw_child_map(key, part):
    key = jax.random.fold_in(key, 9)
    rows_child = U // N_ROW
    blocks = 2 * N_ROW
    block_width = M // blocks
    grid_ratio = N_ROW // N_COL
    heavy_count = 3 * rows_child // (4 * N_ROW)
    light_count = rows_child // N_ROW - heavy_count
    piece_rows = P_SIZE // N_ROW

    def shuffle_group(group_key):
        return jax.random.permutation(group_key, 2 * grid_ratio)

    def spread_rows(row_counts, row_key):
        slots = jnp.repeat(jnp.arange(blocks, dtype=jnp.int32), row_counts, total_repeat_length=rows_child)
        return slots[jax.random.permutation(row_key, rows_child)]

    def shuffle_block(block_key):
        return jax.random.permutation(block_key, block_width)
    members = []
    for sibling in range(2):
        subkey = jax.random.fold_in(key, sibling)
        pattern_key, order_key, place_key = jax.random.split(subkey, 3)
        group_keys = jax.random.split(pattern_key, N_ROW // 2 * N_COL)
        chosen = jax.vmap(shuffle_group)(group_keys).reshape(N_ROW // 2, blocks)
        heavy_even = chosen < grid_ratio
        heavy_mask = jnp.stack([heavy_even, jnp.logical_not(heavy_even)], 1).reshape(N_ROW, blocks)
        counts = jnp.where(heavy_mask, heavy_count, light_count).astype(jnp.int32)
        order_keys = jax.random.split(order_key, N_ROW)
        target = jax.vmap(spread_rows)(counts, order_keys)
        target = target.reshape(N_ROW, U // P_SIZE, piece_rows).transpose(1, 0, 2).reshape(U)
        onehot = (target[:, None] == jnp.arange(blocks, dtype=jnp.int32)[None, :]).astype(jnp.int32)
        slot_rank = jnp.sum(jnp.cumsum(onehot, 0) * onehot, 1) - 1
        place_keys = jax.random.split(place_key, blocks)
        within = jax.vmap(shuffle_block)(place_keys)
        members.append((target * block_width + within[target, slot_rank]).astype(jnp.int32))
    return jnp.stack(members)


def levels(own_key, extent, shards, low, largest):
    loudness, own = 1.0, jax.random.fold_in(own_key, 6)
    for dim, shards_of in shards:
        draws = jnp.exp(jax.random.uniform(jax.random.fold_in(own, dim), (shards_of,), jnp.float32, low / len(shards), largest / len(shards)))
        loudness = loudness * jnp.repeat(draws, extent[dim] // shards_of).reshape([-1 if axis == dim else 1 for axis in range(len(extent))])
    return loudness


def scatter_about(rng, extent, deviation, bound, cuts=(), kind=jnp.bfloat16):
    drawn = deviation * jax.random.normal(rng, extent, jnp.float32)
    if cuts:
        drawn = drawn * levels(rng, extent, cuts, -0.22, 0.18)
    return jnp.clip(drawn, -bound, bound).astype(kind)


def setup_inputs(seed: int = 0) -> dict:
    keys = jax.random.split(jax.random.key(seed), 5)
    children = draw_children(jax.random.fold_in(keys[4], 71), 0)
    pivot_inverse = draw_pivot_inverse(jax.random.fold_in(keys[4], 71), 0)
    parent_front = scatter_about(keys[2], (M, M), 0.1, 1.5, ((0, 32), (1, 8)), jnp.float32)
    child_map = draw_child_map(jax.random.fold_in(keys[4], 71), 0)
    return dict(children=children, pivot_inverse=pivot_inverse, parent_front=parent_front, child_map=child_map)


def to_logical(stored, groups, dimension):
    length = stored.shape[dimension]
    leading = jnp.moveaxis(stored, dimension, 0)
    trailing = leading.shape[1:]
    leading = leading.reshape((groups, length // P_SIZE, P_SIZE // groups) + trailing)
    leading = jnp.swapaxes(leading, 0, 1).reshape((length,) + trailing)
    return jnp.moveaxis(leading, 0, dimension)


def to_stored(logical, groups, dimension):
    length = logical.shape[dimension]
    leading = jnp.moveaxis(logical, dimension, 0)
    trailing = leading.shape[1:]
    leading = leading.reshape((length // P_SIZE, groups, P_SIZE // groups) + trailing)
    leading = jnp.swapaxes(leading, 0, 1).reshape((length,) + trailing)
    return jnp.moveaxis(leading, 0, dimension)


def factor_child(stored, inverses):
    matrix = to_logical(to_logical(stored, N_ROW, 0), N_COL, 1)
    factor = jnp.zeros((F, S), jnp.bfloat16)
    for panel_index in range(NPAN):
        offset = panel_index * P_SIZE
        column_block = matrix[offset:, offset:offset + P_SIZE].astype(jnp.bfloat16)
        left_all = lax.dot_general(column_block, inverses[panel_index], (((1,), (1,)), ((), ())), preferred_element_type=jnp.float32).astype(jnp.bfloat16)
        factor = factor.at[offset:, offset:offset + P_SIZE].set(left_all)
        widened = left_all[P_SIZE:].astype(jnp.float32)
        update = jnp.dot(widened, widened.T, precision=lax.Precision.HIGHEST, preferred_element_type=jnp.float32)
        matrix = matrix.at[offset + P_SIZE:, offset + P_SIZE:].add(-update)
    schur = matrix[S:, S:].astype(jnp.bfloat16)
    return to_stored(to_stored(factor, N_ROW, 0), N_COL, 1), schur


def reference(children, pivot_inverse, parent_front, child_map):
    parent = parent_front
    factors = []
    for sibling in range(2):
        factor, schur = factor_child(children[sibling], pivot_inverse[sibling])
        factors.append(factor)
        spread = jnp.zeros((M, U), jnp.float32).at[child_map[sibling]].set(schur.astype(jnp.float32))
        parent = parent.at[:, child_map[sibling]].add(spread)
    return parent, jnp.stack(factors)
```

```python
import functools

import jax
import jax.numpy as jnp
from jax import lax
from jax.experimental import pallas as pl
from jax.experimental.pallas import tpu as pltpu
from jax.sharding import PartitionSpec as P

MESH = pl.DeviceIdType.MESH
BF = jnp.bfloat16
F32 = jnp.float32
NPAN = 3
PANEL = 1024
LOCAL_ROWS, LOCAL_COLS = 768, 1536
ROW_PIECE, COL_PIECE = 64, 128
SCHUR_ROWS, SCHUR_COLS = 576, 1152
OUT_ROWS, OUT_COLS = 384, 1536
ROW_SLOT = 32
COL_SLOT = 144
PARTS = (48, 48, 32, 16)
PART_AT = (0, 48, 96, 128)
INV_COLS = 640
N_SEMS = 450
NT = (((1,), (1,)), ((), ()))


def dot(a, b):
    return jnp.dot(a, b, preferred_element_type=F32)


def dot_nt(a, b):
    return lax.dot_general(a, b, NT, preferred_element_type=F32)


class Net:
    def __init__(self, send_sems, recv_sems):
        self.send_sems, self.recv_sems = send_sems, recv_sems
        self.count, self.pending = 0, []

    def copy(self, index, src, dst, device):
        return pltpu.make_async_remote_copy(
            src_ref=src,
            dst_ref=dst,
            send_sem=self.send_sems.at[index],
            recv_sem=self.recv_sems.at[index],
            device_id=device,
            device_id_type=MESH,
        )

    def send(self, src, dst, device):
        index = self.count
        self.count += 1
        copy = self.copy(index, src, dst, device)
        copy.start()
        self.pending.append(copy)
        return index

    def recv(self, index, region, device):
        self.copy(index, region, region, device).wait_recv()

    def drain(self):
        for copy in self.pending:
            copy.wait_send()
        self.pending = []


def ring4(net, region, me, device, then):
    up, down, far = lax.rem(me + 1, 4), lax.rem(me + 3, 4), lax.rem(me + 2, 4)
    ids = {}
    ids["a"] = net.send(region(me, None), region(me, None), device(up))
    ids["b"] = net.send(region(me, None), region(me, None), device(down))

    def from_down():
        net.recv(ids["a"], region(down, None), device(up))
        ids["c"] = net.send(region(down, 0), region(down, 0), device(up))
        then(1, down)

    def from_up():
        net.recv(ids["b"], region(up, None), device(down))
        ids["d"] = net.send(region(up, 1), region(up, 1), device(down))
        then(2, up)

    def far_first():
        net.recv(ids["c"], region(far, 0), device(up))

    def far_second():
        net.recv(ids["d"], region(far, 1), device(down))
        then(3, far)

    return [from_down, from_up, far_first, far_second]


GRID_ORDER = (
    ("A", 1, 0), ("A", 1, 1), ("A", 1, 2), ("A", 1, 3), ("a", 0, 0), ("a", 0, 1), ("a", 1, 0),
    ("a", 1, 1), ("a", 2, 0), ("a", 2, 1), ("a", 3, 0), ("a", 3, 1), ("a", 0, 2), ("a", 0, 3),
    ("a", 1, 2), ("a", 1, 3), ("a", 2, 2), ("a", 2, 3), ("a", 3, 2), ("a", 3, 3),
)


def gather_grid(net, region, x, y):
    along_x = lambda v: {"row": y * 4 + v}
    along_y = lambda v: {"row": v * 4 + x}
    second = {("a", k): [] for k in range(4)} | {("b", k): [] for k in range(4)}
    done = lambda k, v: None

    def start_a(k, xx):
        second["a", k] += ring4(net, lambda v, part: region(v * 4 + xx, 0, part), y, along_y, done)

    def start_b(k, yy):
        second["b", k] += ring4(net, lambda v, part: region(yy * 4 + v, 1, part), x, along_x, done)

    first_a = ring4(net, lambda v, part: region(y * 4 + v, 0, part), x, along_x, start_a)
    first_b = ring4(net, lambda v, part: region(v * 4 + x, 1, part), y, along_y, start_b)
    start_a(0, x)
    start_b(0, y)

    def event(group, k, step):
        if group == "A":
            first_a[step]()
        elif group == "B":
            first_b[step]()
        else:
            second[group, k][step]()

    order = [(g, k, step) for way, k, step in GRID_ORDER for g in (way, chr(ord(way) + 1))]
    return [functools.partial(event, *item) for item in order]


def gather_ring8(net, region, me):
    ways = ({"col": lax.rem(me + 1, 8)}, {"col": lax.rem(me + 7, 8)})
    sign = (-1, 1)
    ids = {}
    for way in (0, 1):
        for half in (way, 1 - way):
            ids[way, 0, half] = net.send(region(me, half), region(me, half), ways[way])

    def event(way, step, half):
        block = lax.rem(me + 8 + sign[way] * step, 8)
        net.recv(ids[way, step - 1, half], region(block, half), ways[way])
        if step < 3 or (step == 3 and half == way):
            ids[way, step, half] = net.send(region(block, half), region(block, half), ways[way])

    order = []
    for step in (1, 2, 3):
        for j in (0, 1):
            order += [(0, step, j), (1, step, 1 - j)]
    order += [(0, 4, 0), (1, 4, 1)]
    return [functools.partial(event, *item) for item in order]


def merge(*lists):
    keyed = []
    for which, items in enumerate(lists):
        for i, item in enumerate(items):
            keyed.append(((i + 0.5) / len(items), which, i, item))
    return [item for *_, item in sorted(keyed, key=lambda k: k[:3])]


def run(items):
    for item in items:
        item()


def iota(shape, dim):
    return lax.broadcasted_iota(jnp.int32, shape, dim)


def kernel(
    children, inverse, parent, child_map,
    out, factor,
    a, wr, wc, inv, lr, lc,
    select_cols, select_rows, place_rows, place_cols,
    loan, schur, s1, g, o2, h,
    maps_in, row_parent, col_parent, slot_c, slot_r, rank_r, rank_c, want_r, want_c,
    local_sems, pre_send, pre_recv, send_sems, recv_sems,
):
    front, row, col = lax.axis_index("front"), lax.axis_index("row"), lax.axis_index("col")
    x, y = lax.rem(row, 4), row // 4
    block = front * 16 + row

    def load(i, src, dst):
        copy = pltpu.make_async_copy(src, dst, local_sems.at[i])
        copy.start()
        return copy

    own_rows = lambda ref, b, n: ref.at[pl.ds(pl.multiple_of(b * n, n), n)]
    load_left = load(0, children.at[0, :, pl.ds(0, 128)], a.at[:, pl.ds(0, 128)])
    load_top = load(
        1, children.at[0, pl.ds(0, 64), pl.ds(128, 1408)], a.at[pl.ds(0, 64), pl.ds(128, 1408)]
    )
    load_inv = [
        load(2 + p, inverse.at[0, p], inv.at[p, pl.ds(pl.multiple_of(row * 64, 64), 64)])
        for p in range(NPAN)
    ]

    barrier = pltpu.get_barrier_semaphore()
    for k in range(1, 8):
        pl.semaphore_signal(
            barrier, inc=1, device_id={"col": lax.rem(col + k, 8)}, device_id_type=MESH
        )
    for k in range(1, 32):
        other = lax.rem(block + k, 32)
        pl.semaphore_signal(
            barrier,
            inc=1,
            device_id={"front": other // 16, "row": lax.rem(other, 16)},
            device_id_type=MESH,
        )

    load_rest = load(
        5, children.at[0, pl.ds(64, 704), pl.ds(128, 1408)], a.at[pl.ds(64, 704), pl.ds(128, 1408)]
    )
    load_parent = load(6, parent, out)
    load_maps = load(7, child_map, maps_in)

    net = Net(send_sems, recv_sems)
    lane_c = pl.ds(pl.multiple_of(col * 128, 128), 128)
    rows_r = pl.ds(pl.multiple_of(row * 64, 64), 64)

    def in_block(b, half, part):
        if part is None:
            return pl.ds(pl.multiple_of(b * 64 + half * 32, 32), 32)
        return pl.ds(pl.multiple_of(b * 64 + half * 32 + part * 16, 16), 16)

    def start_ring(p):
        top = p * ROW_PIECE
        half_rows = (LOCAL_ROWS - top) // 2

        def region(b, half):
            return wr.at[
                p,
                pl.ds(top + half * half_rows, half_rows),
                pl.ds(pl.multiple_of(b * 128, 128), 128),
            ]

        return gather_ring8(net, region, col)

    def start_grid(p):
        left = (p + 1) * COL_PIECE

        def region(b, half, part):
            return wc.at[p, in_block(b, half, part), pl.ds(left, LOCAL_COLS - left)]

        return gather_grid(net, region, x, y)

    def lend(p, width):
        to = {"row": (3 - y) * 4 + x}
        return pltpu.make_async_remote_copy(
            src_ref=inv.at[p, rows_r, pl.ds(640, width)],
            dst_ref=loan.at[p, :, pl.ds(0, width)],
            send_sem=pre_send.at[p],
            recv_sem=pre_recv.at[p],
            device_id=to,
            device_id_type=MESH,
        )

    def lend_inverses():
        for p in range(NPAN):
            load_inv[p].wait()

        @pl.when(y == 3)
        def _():
            for p in range(NPAN):
                lend(p, 384).start()

        @pl.when(y == 2)
        def _():
            for p in range(NPAN):
                lend(p, 128).start()

    def start_inverse(p):
        @pl.when(y == 0)
        def _():
            lend(p, 384).wait_recv()
            inv[p, rows_r, 256:640] = loan[p, :, 0:384]

        @pl.when(y == 1)
        def _():
            lend(p, 128).wait_recv()
            inv[p, rows_r, 512:640] = loan[p, :, 0:128]

        def region(b, half, part):
            return inv.at[p, in_block(b, half, part), pl.ds(0, INV_COLS)]

        return gather_grid(net, region, x, y)

    def unfold_inverse(p):
        @pl.when(y == 3)
        def _():
            lend(p, 384).wait_send()

        @pl.when(y == 2)
        def _():
            lend(p, 128).wait_send()

        inv[p, 768:1024, 640:1024] = inv[p, 0:256, 256:640]
        inv[p, 512:768, 640:768] = inv[p, 256:512, 512:640]

    load_left.wait()
    wr[0, :, lane_c] = a[:, 0:128].astype(BF)
    load_top.wait()
    wc[0, rows_r, 128:] = a[0:64, 128:].astype(BF)
    pl.semaphore_wait(barrier, 38)
    ring = start_ring(0)
    grid = start_grid(0)
    lend_inverses()
    inverse_events = start_inverse(0)

    tri = select_cols

    def build_tri(i, carry):
        r0 = pl.multiple_of(i * 128, 128)
        below = iota((128, SCHUR_COLS), 0) + r0 < iota((128, SCHUR_COLS), 1)
        tri[pl.ds(r0, 128), :] = below.astype(F32).astype(BF)
        return carry

    def group_maps():
        load_maps.wait()
        for child in range(2):
            for t in range(9):
                for b in range(16):
                    start = t * PANEL + b * ROW_PIECE
                    row_parent[
                        child * 16 + b : child * 16 + b + 1, t * ROW_PIECE : (t + 1) * ROW_PIECE
                    ] = maps_in[child : child + 1, start : start + ROW_PIECE]
                for b in range(8):
                    start = t * PANEL + b * COL_PIECE
                    col_parent[
                        child * 8 + b : child * 8 + b + 1, t * COL_PIECE : (t + 1) * COL_PIECE
                    ] = maps_in[child : child + 1, start : start + COL_PIECE]

    def make_tri():
        lax.fori_loop(0, SCHUR_COLS // 128, build_tri, 0)

    def as_f(mask):
        return jnp.where(mask, 1.0, 0.0).astype(F32)

    def send_slots_cols():
        mine = col_parent[pl.ds(front * 8 + col, 1), :]
        low = iota((8, SCHUR_COLS), 0) * OUT_COLS
        hot = as_f((mine >= low) & (mine < low + OUT_COLS))
        before = dot(hot.astype(BF), tri[...])
        rank = jnp.sum(hot * before, 0, keepdims=True)
        dest = jnp.sum(hot * iota((8, SCHUR_COLS), 0).astype(F32), 0, keepdims=True)
        part_at, size = PART_AT[0], PARTS[0]
        for j in range(1, len(PARTS)):
            later = as_f(rank >= PART_AT[j])
            part_at = part_at + later * (PART_AT[j] - PART_AT[j - 1])
            size = size + later * (PARTS[j] - PARTS[j - 1])
        slot = rank + 7.0 * part_at + dest * size
        slot_c[...] = jnp.broadcast_to(slot, (8, SCHUR_COLS))

    def send_slots_rows():
        mine = row_parent[pl.ds(front * 16 + row, 1), :]
        low = iota((32, SCHUR_ROWS), 0) * OUT_ROWS
        hot = as_f((mine >= low) & (mine < low + OUT_ROWS))
        before = dot(hot.astype(BF), tri[0:SCHUR_ROWS, 0:SCHUR_ROWS])
        rank = jnp.sum(hot * before, 0, keepdims=True)
        dest = jnp.sum(hot * iota((32, SCHUR_ROWS), 0).astype(F32), 0, keepdims=True)
        slot_r[...] = jnp.broadcast_to(dest * ROW_SLOT + rank, (8, SCHUR_ROWS))

    def receive_ranks():
        low = block * OUT_ROWS
        there = row_parent[...]
        here = as_f((there >= low) & (there < low + OUT_ROWS))
        before = dot(here.astype(BF), tri[0:SCHUR_ROWS, 0:SCHUR_ROWS])
        rank_r[...] = jnp.where(here > 0.5, before, -1.0)
        low_c = col * OUT_COLS
        there = col_parent[...]
        here = as_f((there >= low_c) & (there < low_c + OUT_COLS))
        before = dot(here.astype(BF), tri[...])
        rank_c[...] = jnp.where(here > 0.5, before, -1.0)

    def wanted_rows(i, carry):
        rank = rank_r[pl.ds(i, 1), :]
        value = (row_parent[pl.ds(i, 1), :] - block * OUT_ROWS + 1).astype(F32)
        match = rank == iota((ROW_SLOT, SCHUR_ROWS), 0).astype(F32)
        want = jnp.sum(jnp.where(match, value, 0.0), 1, keepdims=True) - 1.0
        want_r[pl.ds(pl.multiple_of(i * ROW_SLOT, ROW_SLOT), ROW_SLOT), :] = jnp.broadcast_to(
            want, (ROW_SLOT, 128)
        )
        return carry

    def wanted_cols(i, carry):
        rank = rank_c[pl.ds(i, 1), :]
        value = (col_parent[pl.ds(i, 1), :] - col * OUT_COLS + 1).astype(F32)
        match = rank == iota((COL_SLOT, SCHUR_COLS), 0).astype(F32)
        want = jnp.sum(jnp.where(match, value, 0.0), 1, keepdims=True) - 1.0
        child, source = i // 8, lax.rem(i, 8)
        for size, start in zip(PARTS, PART_AT):
            at = child * SCHUR_COLS + 8 * start + source * size
            want_c[pl.ds(pl.multiple_of(at, 16), size), :] = jnp.broadcast_to(
                want[start : start + size], (size, 128)
            )
        return carry

    def make_wanted_rows():
        lax.fori_loop(0, 32, wanted_rows, 0)

    def make_wanted_cols():
        lax.fori_loop(0, 16, wanted_cols, 0)

    def build_select_cols(i, carry):
        r0 = pl.multiple_of(i * 128, 128)
        hit = slot_c[0:1, :] == (iota((128, SCHUR_COLS), 0) + r0).astype(F32)
        select_cols[pl.ds(r0, 128), :] = as_f(hit).astype(BF)
        return carry

    def build_select_rows(i, carry):
        r0 = pl.multiple_of(i * 128, 128)
        hit = slot_r[0:1, :] == (iota((128, SCHUR_ROWS), 0) + r0).astype(F32)
        select_rows[pl.ds(r0, 128), :] = as_f(hit).astype(BF)
        return carry

    def build_place_rows(i, carry):
        r0 = pl.multiple_of(i * 128, 128)
        hit = want_r[pl.ds(r0, 128), 0:1] == iota((128, OUT_ROWS), 1).astype(F32)
        child, at = i // 4, pl.multiple_of(lax.rem(i, 4) * 128, 128)
        place_rows[child, :, pl.ds(at, 128)] = as_f(hit).T.astype(BF)
        return carry

    def build_place_cols(i, carry):
        r0 = pl.multiple_of(i * 128, 128)
        hit = want_c[pl.ds(r0, 128), 0:1] == iota((128, OUT_COLS), 1).astype(F32)
        place_cols[pl.ds(r0, 128), :] = as_f(hit).astype(BF)
        return carry

    def make_selects():
        lax.fori_loop(0, SCHUR_COLS // 128, build_select_cols, 0)
        lax.fori_loop(0, 8, build_select_rows, 0)

    def make_place_rows():
        lax.fori_loop(0, 8, build_place_rows, 0)

    def make_place_cols(part):
        lax.fori_loop(part * 6, part * 6 + 6, build_place_cols, 0)

    maps = [
        group_maps, make_tri, send_slots_cols, send_slots_rows, receive_ranks, make_wanted_rows,
        make_wanted_cols, make_selects, make_place_rows,
    ] + [functools.partial(make_place_cols, part) for part in range(3)]

    def left_rows(p, i):
        top = p * ROW_PIECE
        tile, depth = pl.ds(i * 256, 256), pl.ds(0, (i + 1) * 256)
        lr[top:, tile] = dot_nt(wr[p, top:, depth], inv[p, tile, depth]).astype(BF)

    def left_cols(p, i):
        left = (p + 1) * COL_PIECE
        tile, depth = pl.ds(i * 256, 256), pl.ds(0, (i + 1) * 256)
        lc[tile, left:] = dot(inv[p, tile, depth], wc[p, depth, left:]).astype(BF)

    def left_work(p):
        return [functools.partial(f, p, i) for f in (left_rows, left_cols) for i in range(4)]

    def keep_factor(p):
        top = p * ROW_PIECE
        at = slice(p * COL_PIECE, (p + 1) * COL_PIECE)
        factor[top:, at] = lr[top:, lane_c]
        if p:
            factor[:top, at] = jnp.zeros((top, COL_PIECE), BF)

    def next_column(q):
        top, left = q * ROW_PIECE, q * COL_PIECE
        right = left + COL_PIECE
        piece = a[top:, left:right] - dot(lr[top:, :], lc[:, left:right])
        wr[q, top:, lane_c] = piece.astype(BF)

    def next_row(q):
        top, right = q * ROW_PIECE, (q + 1) * COL_PIECE
        piece = a[top : top + ROW_PIECE, right:] - dot(lr[top : top + ROW_PIECE, :], lc[:, right:])
        wc[q, rows_r, right:] = piece.astype(BF)

    def trailing(q, start, stop):
        top = (q + 1) * ROW_PIECE
        a[top:, start:stop] = a[top:, start:stop] - dot(lr[top:, :], lc[:, start:stop])

    def trailing_work(q):
        left = (q + 1) * COL_PIECE
        edges = list(range(left, LOCAL_COLS, 256)) + [LOCAL_COLS]
        return [functools.partial(trailing, q, s, e) for s, e in zip(edges, edges[1:])]

    run(merge(ring, grid, inverse_events, maps))
    load_rest.wait()
    for p in range(NPAN - 1):
        inverse_events = start_inverse(p + 1)
        unfold_inverse(p)
        work = left_work(p)
        run(work)
        next_column(p + 1)
        ring = start_ring(p + 1)
        next_row(p + 1)
        grid = start_grid(p + 1)
        rest = [functools.partial(keep_factor, p)] + trailing_work(p + 1)
        run(merge(ring, grid, inverse_events, rest))
    last = NPAN - 1
    unfold_inverse(last)
    run(left_work(last))
    for start in range(0, SCHUR_COLS, 384):
        at = slice(start, start + 384)
        cols = slice(NPAN * COL_PIECE + start, NPAN * COL_PIECE + start + 384)
        top = NPAN * ROW_PIECE
        schur[:, at] = (a[top:, cols] - dot(lr[top:, :], lc[:, cols])).astype(BF)

    def part_rows(j, b):
        return pl.ds(pl.multiple_of(8 * PART_AT[j] + b * PARTS[j], 16), PARTS[j])

    spans = [pl.ds(8 * start, 8 * size) for start, size in zip(PART_AT, PARTS)]
    sent_z = []
    for j, span in enumerate(spans):
        s1[span, :] = dot_nt(select_cols[span, :], schur[...]).astype(BF)
        ids = []
        for k in (1, 7, 2, 6, 3, 5, 4):
            to = lax.rem(col + k, 8)
            src, dst = s1.at[part_rows(j, to)], g.at[part_rows(j, col)]
            ids.append((k, net.send(src, dst, {"col": to})))
        g[part_rows(j, col), :] = s1[part_rows(j, col), :]
        sent_z.append(ids)
    keep_factor(last)
    sent_xy = []
    at_row = lambda b: pl.ds(pl.multiple_of(b * ROW_SLOT, ROW_SLOT), ROW_SLOT)
    for j, span in enumerate(spans):
        for k, index in sent_z[j]:
            source = lax.rem(col + 8 - k, 8)
            net.recv(index, g.at[part_rows(j, source)], {"col": source})
        o2[:, span] = dot_nt(select_rows[...], g[span, :]).astype(BF)
        ids = []
        for k in range(1, 32):
            to = lax.rem(block + k, 32)
            device = {"front": to // 16, "row": lax.rem(to, 16)}
            ids.append((k, net.send(o2.at[at_row(to), span], h.at[at_row(block), span], device)))
        h[at_row(block), span] = o2[at_row(block), span]
        sent_xy.append(ids)
    load_parent.wait()
    for j, span in enumerate(spans):
        for k, index in sent_xy[j]:
            source = lax.rem(block + 32 - k, 32)
            device = {"front": source // 16, "row": lax.rem(source, 16)}
            net.recv(index, h.at[at_row(source), span], device)
        for child in range(2):
            rows = dot(place_rows[child], h[pl.ds(child * 512, 512), span]).astype(BF)
            cols = place_cols[pl.ds(child * SCHUR_COLS + 8 * PART_AT[j], 8 * PARTS[j]), :]
            out[...] = out[...] + dot(rows, cols)
    net.drain()


def on_device(children, pivot_inverse, parent_front, child_map):
    vmem = pl.BlockSpec(memory_space=pltpu.VMEM)
    hbm = pl.BlockSpec(memory_space=pl.ANY)
    parent_out, factor = pl.pallas_call(
        kernel,
        out_shape=(
            jax.ShapeDtypeStruct((OUT_ROWS, OUT_COLS), F32),
            jax.ShapeDtypeStruct((LOCAL_ROWS, NPAN * COL_PIECE), BF),
        ),
        in_specs=[hbm, hbm, hbm, hbm],
        out_specs=(vmem, vmem),
        scratch_shapes=[
            pltpu.VMEM((LOCAL_ROWS, LOCAL_COLS), F32),
            pltpu.VMEM((NPAN, LOCAL_ROWS, PANEL), BF),
            pltpu.VMEM((NPAN, PANEL, LOCAL_COLS), BF),
            pltpu.VMEM((NPAN, PANEL, PANEL), BF),
            pltpu.VMEM((LOCAL_ROWS, PANEL), BF),
            pltpu.VMEM((PANEL, LOCAL_COLS), BF),
            pltpu.VMEM((SCHUR_COLS, SCHUR_COLS), BF),
            pltpu.VMEM((32 * ROW_SLOT, SCHUR_ROWS), BF),
            pltpu.VMEM((2, OUT_ROWS, 16 * ROW_SLOT), BF),
            pltpu.VMEM((2 * SCHUR_COLS, OUT_COLS), BF),
            pltpu.VMEM((NPAN, ROW_PIECE, 384), BF),
            pltpu.VMEM((SCHUR_ROWS, SCHUR_COLS), BF),
            pltpu.VMEM((SCHUR_COLS, SCHUR_ROWS), BF),
            pltpu.VMEM((SCHUR_COLS, SCHUR_ROWS), BF),
            pltpu.VMEM((32 * ROW_SLOT, SCHUR_COLS), BF),
            pltpu.VMEM((32 * ROW_SLOT, SCHUR_COLS), BF),
            pltpu.VMEM((2, 9216), jnp.int32),
            pltpu.VMEM((32, SCHUR_ROWS), jnp.int32),
            pltpu.VMEM((16, SCHUR_COLS), jnp.int32),
            pltpu.VMEM((8, SCHUR_COLS), F32),
            pltpu.VMEM((8, SCHUR_ROWS), F32),
            pltpu.VMEM((32, SCHUR_ROWS), F32),
            pltpu.VMEM((16, SCHUR_COLS), F32),
            pltpu.VMEM((32 * ROW_SLOT, 128), F32),
            pltpu.VMEM((2 * SCHUR_COLS, 128), F32),
            pltpu.SemaphoreType.DMA((8,)),
            pltpu.SemaphoreType.DMA((NPAN,)),
            pltpu.SemaphoreType.DMA((NPAN,)),
            pltpu.SemaphoreType.DMA((N_SEMS,)),
            pltpu.SemaphoreType.DMA((N_SEMS,)),
        ],
        compiler_params=pltpu.CompilerParams(
            collective_id=0, has_side_effects=True, vmem_limit_bytes=62 * 2**20
        ),
    )(
        children,
        pivot_inverse,
        parent_front,
        child_map,
    )
    return parent_out, factor[None]


def solution(mesh):
    in_specs = (
        P("front", "row", "col"),
        P("front", None, "row", None),
        P(("front", "row"), "col"),
        P(),
    )
    out_specs = (P(("front", "row"), "col"), P("front", "row", "col"))
    return jax.shard_map(
        on_device, mesh=mesh, in_specs=in_specs, out_specs=out_specs, check_vma=False
    )
```
